256 devices in a mesh: ctx: 16 (over z, x_hi), tp: 16 (over x_lo, y, core).
Axes of the slice: x: 4 (x_hi: 2, x_lo: 2; x = x_hi * 2 + x_lo), y: 4, z: 8, core: 2. Of those that a mesh axis runs over, the one named last changes fastest.
Arguments:
- query_feat: bfloat16 [4096, 4096], P('ctx', 'tp'), may hold values from -6 to 6
- key_feat: bfloat16 [4096, 4096], P('ctx', 'tp'), may hold values from -6 to 6
- value_feat: bfloat16 [4096, 4096], P('ctx', 'tp'), may hold values from -6 to 6
- residue: float32 [16, 4096], P(None, 'tp'), may hold values from -1.5 to 1.5
- decay_rate: float32 [16, 4096], P(None, 'tp'), may hold values from 1.2207031e-05 to 0.1
- skip_gain: float32 [4096], P('tp'), may hold values from 0.5 to 1.5
- out_weight: bfloat16 [4096, 4096], P('tp'), may hold values from -0.09375 to 0.09375
- cotangent: bfloat16 [4096, 4096], P('ctx', 'tp'), may hold values from -6 to 6
Outputs:
- layer_out: bfloat16 [4096, 4096], P('ctx', 'tp')
- grad_query: bfloat16 [4096, 4096], P('ctx', 'tp')
- grad_key: bfloat16 [4096, 4096], P('ctx', 'tp')
- grad_value: bfloat16 [4096, 4096], P('ctx', 'tp')
- grad_out_weight: float32 [4096, 4096], P('tp', 'ctx')
The draws below stay inside these ranges and needn't reach their ends.
All inputs are finite; a program needn't handle non-finite values.
Results may differ from the reference program's by a relative error of at most 0.019.
Values may be sent and summed in bfloat16 or wider, within the bound.
No kernel may reach another device: no remote copies, remote signals or barrier semaphores. Data moves between devices by JAX's collectives and lax.ppermute only.
A program may use at most 128 MiB of HBM per device.

```python
import math
import jax
import jax.numpy as jnp
from jax import lax

D = 4096
MODES = 16
LENGTH = 4096


def steps_of(rng, extent, pieces, low, high):
    level, own = 1.0, jax.random.fold_in(rng, 6)
    for dim, blocks in pieces:
        steps = jnp.exp(jax.random.uniform(jax.random.fold_in(own, dim), (blocks,), jnp.float32, low / len(pieces), high / len(pieces)))
        level = level * jnp.repeat(steps, extent[dim] // blocks).reshape([-1 if axis == dim else 1 for axis in range(len(extent))])
    return level


def scatter_about(stream_key, extent, scale, most, shards=(), kind=jnp.bfloat16):
    result = jax.random.normal(stream_key, extent, jnp.float32) * scale
    if len(shards) > 0:
        result = steps_of(stream_key, extent, shards, -0.22, 0.18) * result
    return jnp.clip(result, min=-most, max=most).astype(kind)


def setup_inputs(seed: int = 0) -> dict:
    arg_keys = jax.random.split(jax.random.key(seed), 9)
    query_feat = scatter_about(arg_keys[0], (LENGTH, D), 1.0, 6.0, ((0, 16), (1, 16)))
    key_feat = scatter_about(arg_keys[1], (LENGTH, D), 1.0, 6.0, ((0, 16), (1, 16)))
    value_feat = scatter_about(arg_keys[2], (LENGTH, D), 1.0, 6.0, ((0, 16), (1, 16)))
    residue = scatter_about(arg_keys[3], (MODES, D), 0.25, 1.5, ((1, 16),), jnp.float32)
    decay_rate = jnp.clip(jnp.exp(math.log(0.1) - 9.010913 * jax.random.uniform(arg_keys[4], (MODES, D), jnp.float32) ** steps_of(arg_keys[4], (MODES, D), ((1, 16),), -0.2, 0.2)), 1.220703143189894e-05, 0.1)
    skip_gain = jnp.clip(0.5 + 1.0 * jax.random.uniform(arg_keys[5], (D,), jnp.float32) ** steps_of(arg_keys[5], (D,), ((0, 16),), -0.2, 0.2), 0.5, 1.5)
    out_weight = scatter_about(arg_keys[6], (D, D), D ** -0.5, 0.09375, ((0, 16),))
    cotangent = scatter_about(arg_keys[7], (LENGTH, D), 1.0, 6.0, ((0, 16), (1, 16)))
    return {"query_feat": query_feat, "key_feat": key_feat, "value_feat": value_feat, "residue": residue, "decay_rate": decay_rate, "skip_gain": skip_gain, "out_weight": out_weight, "cotangent": cotangent}


highest = lax.Precision.HIGHEST

def modal_tables(rates, coefficient, block_len):
    offsets = jnp.arange(block_len, dtype=jnp.float32)
    powers = jnp.exp(-rates[None] * offsets[:, None, None])
    impulse = jnp.einsum('jnc,nc->jc', powers, coefficient, precision=highest)
    spread = jnp.arange(block_len)[:, None] - jnp.arange(block_len)[None, :]
    toeplitz = jnp.where((spread >= 0)[:, :, None], jnp.take(impulse, jnp.maximum(spread, 0).astype(jnp.int32), axis=0), jnp.float32(0.0))
    tail_table = powers[::-1]
    head_table = coefficient[None] * powers * jnp.exp(-rates)[None]
    return (toeplitz, tail_table, head_table)

def long_filter(signal, rates, coefficient):
    length, channels = signal.shape
    block_len = 64
    block_count = length // block_len
    toeplitz, tail_table, head_table = modal_tables(rates, coefficient, block_len)
    across = jnp.exp(-rates * block_len)

    def advance(modal_state, segment):
        inner_part = jnp.einsum('tsc,sc->tc', toeplitz, segment, precision=highest)
        inner_part = inner_part + jnp.einsum('tnc,nc->tc', head_table, modal_state, precision=highest)
        modal_state = across * modal_state + jnp.einsum('snc,sc->nc', tail_table, segment, precision=highest)
        return (modal_state, inner_part)
    start_state = jnp.zeros(rates.shape, jnp.float32)
    _, filtered_blocks = lax.scan(advance, start_state, signal.reshape(block_count, block_len, channels))
    return filtered_blocks.reshape(length, channels)

def reference(query_feat, key_feat, value_feat, residue, decay_rate, skip_gain, out_weight, cotangent):
    queries = query_feat.astype(jnp.float32)
    key_rows = key_feat.astype(jnp.float32)
    value_rows = value_feat.astype(jnp.float32)
    coefficient = residue * jnp.sqrt(-jnp.expm1(-2.0 * decay_rate))
    signal = key_rows * value_rows
    filtered = long_filter(signal, decay_rate, coefficient) + skip_gain[None] * signal
    product = (queries * filtered).astype(jnp.bfloat16)
    weight_full = out_weight.astype(jnp.float32)
    product_full = product.astype(jnp.float32)
    cot_full = cotangent.astype(jnp.float32)
    layer_out = jnp.dot(product_full, weight_full, precision=highest).astype(jnp.bfloat16)
    grad_product = jnp.dot(cot_full, weight_full.T, precision=highest)
    grad_out_weight = jnp.dot(product_full.T, cot_full, precision=highest)
    grad_query = (grad_product * filtered).astype(jnp.bfloat16)
    grad_filtered = grad_product * queries
    grad_long = long_filter(grad_filtered[::-1], decay_rate, coefficient)[::-1]
    grad_signal = skip_gain[None] * grad_filtered + grad_long
    grad_key = (grad_signal * value_rows).astype(jnp.bfloat16)
    grad_value = (grad_signal * key_rows).astype(jnp.bfloat16)
    return (layer_out, grad_query, grad_key, grad_value, grad_out_weight)
```

```python
import jax
import jax.numpy as jnp
from jax import lax
from jax.experimental import pallas as pl
from jax.experimental.pallas import tpu as pltpu
from jax.sharding import PartitionSpec as P

CHUNKS = 8
LANES = 128
F32 = jnp.float32
BF16 = jnp.bfloat16
VMEM_LIMIT = 32 * 1024 * 1024


def row_index(shape):
    return lax.broadcasted_iota(jnp.int32, shape, 0)


def lane_groups(channels):
    return [(group, pl.ds(group * LANES, LANES)) for group in range(channels // LANES)]


def chunk_pass(x_ref, rate_ref, entering_ref, total_ref, backward):
    rows = x_ref.shape[1]
    modes, channels = rate_ref.shape
    chunk_len = rows // CHUNKS
    for group, lanes in lane_groups(channels):
        rates = [jnp.broadcast_to(rate_ref[n : n + 1, lanes], (CHUNKS, LANES)) for n in range(modes)]
        decays = [jnp.exp(-rate) for rate in rates]

        def advance(step, states):
            j = chunk_len - 1 - step if backward else step
            x = x_ref[group, pl.ds(j, CHUNKS, stride=chunk_len), :]
            return tuple(d * s + x for d, s in zip(decays, states))

        zero = jnp.zeros((CHUNKS, LANES), F32)
        states = lax.fori_loop(0, chunk_len, advance, (zero,) * modes, unroll=4)
        chunk = row_index((CHUNKS, LANES))
        order = CHUNKS - 1 - chunk if backward else chunk
        for n in range(modes):
            total = states[n]
            span = 1
            while span < CHUNKS:
                earlier = pltpu.roll(total, CHUNKS - span if backward else span, 0)
                across = jnp.exp(-rates[n] * (chunk_len * span))
                total = total + jnp.where(order >= span, across * earlier, 0.0)
                span *= 2
            entering = pltpu.roll(total, CHUNKS - 1 if backward else 1, 0)
            entering_ref[n, :, lanes] = jnp.where(order >= 1, entering, 0.0)
            last = 0 if backward else CHUNKS - 1
            total_ref[n : n + 1, lanes] = total[last : last + 1, :]


def incoming_state(states_ref, rate_ref, place, rows, backward):
    devices = states_ref.shape[0]
    across = jnp.exp(-rate_ref[...] * rows)
    state = jnp.zeros(rate_ref.shape, F32)
    for step in range(devices):
        k = devices - 1 - step if backward else step
        ahead = (k > place) if backward else (k < place)
        state = jnp.where(ahead, across * state + states_ref[k], state)
    return state


def filter_pass(x_ref, y_ref, rate_ref, coefficient_ref, skip_ref, entering_ref, incoming_ref, backward):
    rows = x_ref.shape[1]
    modes, channels = rate_ref.shape
    chunk_len = rows // CHUNKS
    for group, lanes in lane_groups(channels):
        chunk = row_index((CHUNKS, LANES))
        order = CHUNKS - 1 - chunk if backward else chunk
        start = (order * chunk_len).astype(F32)
        decays, weights, states = [], [], []
        for n in range(modes):
            rate = jnp.broadcast_to(rate_ref[n : n + 1, lanes], (CHUNKS, LANES))
            decays.append(jnp.exp(-rate))
            weights.append(jnp.broadcast_to(coefficient_ref[n : n + 1, lanes], (CHUNKS, LANES)))
            outer = jnp.broadcast_to(incoming_ref[n : n + 1, lanes], (CHUNKS, LANES))
            states.append(entering_ref[n, :, lanes] + jnp.exp(-rate * start) * outer)
        skip = jnp.broadcast_to(skip_ref[0:1, lanes], (CHUNKS, LANES))

        def advance(step, states):
            j = chunk_len - 1 - step if backward else step
            x = x_ref[group, pl.ds(j, CHUNKS, stride=chunk_len), :]
            states = tuple(d * s + x for d, s in zip(decays, states))
            terms = [w * s for w, s in zip(weights, states)] + [skip * x]
            while len(terms) > 1:
                pairs = [terms[i] + terms[i + 1] for i in range(0, len(terms) - 1, 2)]
                terms = pairs + (terms[-1:] if len(terms) % 2 else [])
            y_ref[group, pl.ds(j, CHUNKS, stride=chunk_len), :] = terms[0]
            return states

        lax.fori_loop(0, chunk_len, advance, tuple(states), unroll=2)


def dot(a, b, a_dim, b_dim):
    return lax.dot_general(a, b, (((a_dim,), (b_dim,)), ((), ())), preferred_element_type=F32)


def signal_kernel(key_ref, value_ref, rate_ref, entering_ref, send_ref, x_ref, total_ref):
    for group, lanes in lane_groups(key_ref.shape[1]):
        x_ref[group] = key_ref[:, lanes].astype(F32) * value_ref[:, lanes].astype(F32)
    chunk_pass(x_ref, rate_ref, entering_ref, total_ref, False)
    for k in range(send_ref.shape[0]):
        send_ref[k] = total_ref[...]


def middle_kernel(
    place_ref, query_ref, key_ref, value_ref, rate_ref, coefficient_ref, skip_ref, entering_ref, states_ref,
    pieces_ref, weight_ref,
    product_ref, grad_query_ref, grad_filtered_ref, back_entering_ref, back_send_ref,
    x_ref, y_ref, incoming_ref, total_ref,
):
    rows, channels = key_ref.shape
    for group, lanes in lane_groups(channels):
        x_ref[group] = key_ref[:, lanes].astype(F32) * value_ref[:, lanes].astype(F32)
    incoming_ref[...] = incoming_state(states_ref, rate_ref, place_ref[0], rows, False)
    filter_pass(x_ref, y_ref, rate_ref, coefficient_ref, skip_ref, entering_ref, incoming_ref, False)
    for group, lanes in lane_groups(channels):
        product_ref[:, lanes] = (query_ref[:, lanes].astype(F32) * y_ref[group]).astype(BF16)
    grad_rows = jnp.zeros((rows, channels), F32)
    width = pieces_ref.shape[2]
    for b in range(pieces_ref.shape[0]):
        grad_rows = grad_rows + dot(pieces_ref[b], weight_ref[:, b * width : (b + 1) * width], 1, 1)
    for group, lanes in lane_groups(channels):
        part = grad_rows[:, group * LANES : (group + 1) * LANES]
        grad_query_ref[:, lanes] = (part * y_ref[group]).astype(BF16)
        grad_filtered_ref[group] = part * query_ref[:, lanes].astype(F32)
    chunk_pass(grad_filtered_ref, rate_ref, back_entering_ref, total_ref, True)
    for k in range(back_send_ref.shape[0]):
        back_send_ref[k] = total_ref[...]


def update_kernel(product_ref, pieces_ref, out_ref):
    turned = product_ref[...].astype(F32).T.astype(BF16)
    for b in range(out_ref.shape[0]):
        out_ref[b] = dot(turned, pieces_ref[b], 1, 0).astype(BF16)


def share_kernel(product_ref, weight_ref, out_ref):
    width = out_ref.shape[2]
    product = product_ref[...]
    for b in range(out_ref.shape[0]):
        out_ref[b] = dot(product, weight_ref[:, b * width : (b + 1) * width], 1, 0).astype(BF16)


def back_kernel(
    place_ref, key_ref, value_ref, rate_ref, coefficient_ref, skip_ref, entering_ref, states_ref, grad_filtered_ref,
    grad_key_ref, grad_value_ref,
    y_ref, incoming_ref,
):
    rows, channels = key_ref.shape
    incoming_ref[...] = incoming_state(states_ref, rate_ref, place_ref[0], rows, True)
    filter_pass(grad_filtered_ref, y_ref, rate_ref, coefficient_ref, skip_ref, entering_ref, incoming_ref, True)
    for group, lanes in lane_groups(channels):
        grad_key_ref[:, lanes] = (y_ref[group] * value_ref[:, lanes].astype(F32)).astype(BF16)
        grad_value_ref[:, lanes] = (y_ref[group] * key_ref[:, lanes].astype(F32)).astype(BF16)


def call(kernel, out_shape, scratch=(), scalar=False, count=1, flops=0, bytes_accessed=1 << 20):
    vmem = pl.BlockSpec(memory_space=pltpu.VMEM)
    smem = pl.BlockSpec(memory_space=pltpu.SMEM)
    return pl.pallas_call(
        kernel,
        out_shape=out_shape,
        in_specs=([smem] if scalar else []) + [vmem] * count,
        out_specs=[vmem] * len(out_shape),
        scratch_shapes=list(scratch),
        compiler_params=pltpu.CompilerParams(vmem_limit_bytes=VMEM_LIMIT),
        cost_estimate=pl.CostEstimate(flops=flops, bytes_accessed=bytes_accessed, transcendentals=0),
    )


def on_device(query_feat, key_feat, value_feat, residue, decay_rate, skip_gain, out_weight, cotangent):
    rows, channels = query_feat.shape
    modes = decay_rate.shape[0]
    ctx, tp = lax.axis_size("ctx"), lax.axis_size("tp")
    place = lax.axis_index("ctx").astype(jnp.int32).reshape(1)
    shape = jax.ShapeDtypeStruct
    block = pltpu.VMEM((channels // LANES, rows, LANES), F32)
    state = pltpu.VMEM((modes, channels), F32)
    entering_shape = shape((modes, CHUNKS, channels), F32)
    send_shape = shape((ctx, modes, channels), F32)
    matmul_flops = 2 * rows * channels * out_weight.shape[1]

    coefficient = residue * jnp.sqrt(-jnp.expm1(-2.0 * decay_rate))
    skip = skip_gain.reshape(1, channels)

    entering, send = call(signal_kernel, [entering_shape, send_shape], [block, state], count=3, flops=1 << 25)(
        key_feat, value_feat, decay_rate
    )
    states = lax.all_to_all(send, "ctx", 0, 0)
    pieces = lax.all_gather(cotangent, "tp", axis=0)

    product, grad_query, grad_filtered, back_entering, back_send = call(
        middle_kernel,
        [
            shape((rows, channels), BF16),
            shape((rows, channels), BF16),
            shape((channels // LANES, rows, LANES), F32),
            entering_shape,
            send_shape,
        ],
        [block, block, state, state],
        scalar=True,
        count=10,
        flops=matmul_flops + (1 << 26),
        bytes_accessed=6 << 20,
    )(
        place, query_feat, key_feat, value_feat, decay_rate, coefficient, skip, entering, states, pieces, out_weight
    )
    back_states = lax.all_to_all(back_send, "ctx", 0, 0)

    (update,) = call(
        update_kernel, [shape((ctx, channels, channels), BF16)], count=2, flops=matmul_flops, bytes_accessed=4 << 20
    )(product, pieces)
    updates = lax.all_to_all(update, "ctx", 0, 0)
    (share,) = call(
        share_kernel, [shape((tp, rows, channels), BF16)], count=2, flops=matmul_flops, bytes_accessed=4 << 20
    )(product, out_weight)
    shares = lax.all_to_all(share, "tp", 0, 0)

    grad_key, grad_value = call(
        back_kernel,
        [shape((rows, channels), BF16), shape((rows, channels), BF16)],
        [block, state],
        scalar=True,
        count=8,
        flops=1 << 26,
        bytes_accessed=2 << 20,
    )(place, key_feat, value_feat, decay_rate, coefficient, skip, back_entering, back_states, grad_filtered)

    layer_out = jnp.sum(shares.astype(F32), axis=0).astype(BF16)
    grad_out_weight = jnp.sum(updates.astype(F32), axis=0)
    return (layer_out, grad_query, grad_key, grad_value, grad_out_weight)


def solution(mesh):
    in_specs = (
        P("ctx", "tp"),
        P("ctx", "tp"),
        P("ctx", "tp"),
        P(None, "tp"),
        P(None, "tp"),
        P("tp"),
        P("tp", None),
        P("ctx", "tp"),
    )
    out_specs = (P("ctx", "tp"), P("ctx", "tp"), P("ctx", "tp"), P("ctx", "tp"), P("tp", "ctx"))
    return jax.shard_map(on_device, mesh=mesh, in_specs=in_specs, out_specs=out_specs, check_vma=False)
```

```python
import jax
import jax.numpy as jnp
from jax import lax
from jax.experimental import pallas as pl
from jax.experimental.pallas import tpu as pltpu
from jax.sharding import PartitionSpec as P

CHUNKS = 8
LANES = 128
F32 = jnp.float32
BF16 = jnp.bfloat16
VMEM_LIMIT = 12 * 1024 * 1024


def row_index(shape):
    return lax.broadcasted_iota(jnp.int32, shape, 0)


def lane_groups(channels):
    return [(group, pl.ds(group * LANES, LANES)) for group in range(channels // LANES)]


def one_minus_exp(x):
    series = jnp.ones_like(x)
    for k in range(8, 1, -1):
        series = 1.0 - x / k * series
    return jnp.where(x < 0.3, x * series, 1.0 - jnp.exp(-x))


def chunk_pass(x_ref, rate_ref, entering_ref, total_ref, backward):
    rows = x_ref.shape[1]
    modes, channels = rate_ref.shape
    chunk_len = rows // CHUNKS
    for group, lanes in lane_groups(channels):
        rates = [jnp.broadcast_to(rate_ref[n : n + 1, lanes], (CHUNKS, LANES)) for n in range(modes)]
        decays = [jnp.exp(-rate) for rate in rates]

        def advance(step, states):
            j = chunk_len - 1 - step if backward else step
            x = x_ref[group, pl.ds(j, CHUNKS, stride=chunk_len), :]
            return tuple(d * s + x for d, s in zip(decays, states))

        zero = jnp.zeros((CHUNKS, LANES), F32)
        states = lax.fori_loop(0, chunk_len, advance, (zero,) * modes, unroll=4)
        chunk = row_index((CHUNKS, LANES))
        order = CHUNKS - 1 - chunk if backward else chunk
        for n in range(modes):
            total = states[n]
            span = 1
            while span < CHUNKS:
                earlier = pltpu.roll(total, CHUNKS - span if backward else span, 0)
                across = jnp.exp(-rates[n] * (chunk_len * span))
                total = total + jnp.where(order >= span, across * earlier, 0.0)
                span *= 2
            entering = pltpu.roll(total, CHUNKS - 1 if backward else 1, 0)
            entering_ref[n, :, lanes] = jnp.where(order >= 1, entering, 0.0)
            last = 0 if backward else CHUNKS - 1
            total_ref[n : n + 1, lanes] = total[last : last + 1, :]


def position():
    at_ctx, at_tp = lax.axis_index("ctx"), lax.axis_index("tp")
    return at_ctx // 2, at_ctx % 2, at_tp % 2


def pair_total(total, other, rate, rows, half, backward):
    across = jnp.exp(-rate * rows)
    first = half == (1 if backward else 0)
    return jnp.where(first, across * total + other, across * other + total)


def incoming_state(totals_ref, other, rate, rows, place, half, backward):
    pairs = totals_ref.shape[0]
    across = jnp.exp(-rate * (2 * rows))
    state = jnp.zeros(rate.shape, F32)
    for step in range(pairs):
        k = pairs - 1 - step if backward else step
        ahead = (k > place) if backward else (k < place)
        state = jnp.where(ahead, across * state + totals_ref[k], state)
    first = half == (1 if backward else 0)
    return jnp.where(first, state, jnp.exp(-rate * rows) * state + other)


def filter_pass(x_ref, y_ref, rate_ref, coefficient_ref, skip_ref, entering_ref, incoming_ref, backward):
    rows = x_ref.shape[1]
    modes, channels = rate_ref.shape
    chunk_len = rows // CHUNKS
    for group, lanes in lane_groups(channels):
        chunk = row_index((CHUNKS, LANES))
        order = CHUNKS - 1 - chunk if backward else chunk
        start = (order * chunk_len).astype(F32)
        decays, weights, states = [], [], []
        for n in range(modes):
            rate = jnp.broadcast_to(rate_ref[n : n + 1, lanes], (CHUNKS, LANES))
            decays.append(jnp.exp(-rate))
            weights.append(jnp.broadcast_to(coefficient_ref[n : n + 1, lanes], (CHUNKS, LANES)))
            outer = jnp.broadcast_to(incoming_ref[n : n + 1, lanes], (CHUNKS, LANES))
            states.append(entering_ref[n, :, lanes] + jnp.exp(-rate * start) * outer)
        skip = jnp.broadcast_to(skip_ref[0:1, lanes], (CHUNKS, LANES))

        def advance(step, states):
            j = chunk_len - 1 - step if backward else step
            x = x_ref[group, pl.ds(j, CHUNKS, stride=chunk_len), :]
            states = tuple(d * s + x for d, s in zip(decays, states))
            terms = [w * s for w, s in zip(weights, states)] + [skip * x]
            while len(terms) > 1:
                pairs = [terms[i] + terms[i + 1] for i in range(0, len(terms) - 1, 2)]
                terms = pairs + (terms[-1:] if len(terms) % 2 else [])
            y_ref[group, pl.ds(j, CHUNKS, stride=chunk_len), :] = terms[0]
            return states

        lax.fori_loop(0, chunk_len, advance, tuple(states), unroll=2)


def dot(a, b, a_dim, b_dim):
    return lax.dot_general(a, b, (((a_dim,), (b_dim,)), ((), ())), preferred_element_type=F32)


def copies(ref, total_ref):
    for k in range(ref.shape[0]):
        ref[k] = total_ref[...]


def start_copies(sources, targets, sems):
    copies = [pltpu.make_async_copy(a, b, sems.at[i]) for i, (a, b) in enumerate(zip(sources, targets))]
    for copy in copies:
        copy.start()
    return copies


def multiply_signal(x_ref, key, value):
    for group, lanes in lane_groups(key.shape[1]):
        x_ref[group] = key[:, lanes].astype(F32) * value[:, lanes].astype(F32)


def spread_kernel(block_ref, out_ref, sems):
    count = out_ref.shape[0]
    for copy in start_copies([block_ref] * count, [out_ref.at[k] for k in range(count)], sems):
        copy.wait()


def signal_kernel(
    key_hbm, value_hbm, rate_hbm, residue_hbm,
    entering_ref, total_ref, coefficient_ref,
    x_ref, key_ref, value_ref, rate_ref, residue_ref, sems,
):
    copies = start_copies(
        [key_hbm, value_hbm, rate_hbm, residue_hbm], [key_ref, value_ref, rate_ref, residue_ref], sems
    )
    for copy in copies:
        copy.wait()
    coefficient_ref[...] = residue_ref[...] * jnp.sqrt(one_minus_exp(2.0 * rate_ref[...]))
    multiply_signal(x_ref, key_ref, value_ref)
    chunk_pass(x_ref, rate_ref, entering_ref, total_ref, False)


def pair_kernel(rows, total_ref, other_ref, rate_ref, send_ref):
    _, half, _ = position()
    pair = pair_total(total_ref[...], other_ref[...], rate_ref[...], rows, half, False)
    for k in range(send_ref.shape[0]):
        send_ref[k] = pair


def forward_kernel(
    query_hbm, key_hbm, value_hbm, rate_ref, coefficient_ref, skip_ref, entering_ref, other_ref, totals_ref,
    product_ref, turned_ref, filtered_ref,
    x_ref, incoming_ref, query_ref, key_ref, value_ref, sems,
):
    copies = start_copies([key_hbm, value_hbm, query_hbm], [key_ref, value_ref, query_ref], sems)
    rows, channels = key_ref.shape
    place, half, _ = position()
    incoming_ref[...] = incoming_state(totals_ref, other_ref[...], rate_ref[...], rows, place, half, False)
    copies[0].wait()
    copies[1].wait()
    multiply_signal(x_ref, key_ref, value_ref)
    filter_pass(x_ref, filtered_ref, rate_ref, coefficient_ref, skip_ref, entering_ref, incoming_ref, False)
    copies[2].wait()
    for group, lanes in lane_groups(channels):
        product = query_ref[:, lanes].astype(F32) * filtered_ref[group]
        product_ref[:, lanes] = product.astype(BF16)
        turned_ref[lanes, :] = product.T.astype(BF16)


def gradient_kernel(
    query_hbm, weight_hbm, rate_ref, filtered_ref, mine_ref, sibling_ref,
    grad_query_ref, grad_filtered_ref, entering_ref, total_ref,
    query_ref, weight_ref, sems,
):
    copies = start_copies([query_hbm, weight_hbm], [query_ref, weight_ref], sems)
    rows, channels = query_ref.shape
    _, _, core = position()
    for copy in copies:
        copy.wait()
    grad_rows = jnp.zeros((rows, channels), F32)
    width = mine_ref.shape[2]
    for b in range(mine_ref.shape[0]):
        for block_ref, which in ((mine_ref, core), (sibling_ref, 1 - core)):
            features = pl.ds(pl.multiple_of((2 * b + which) * width, width), width)
            grad_rows = grad_rows + dot(block_ref[b], weight_ref[:, features], 1, 1)
    for group, lanes in lane_groups(channels):
        part = grad_rows[:, group * LANES : (group + 1) * LANES]
        grad_query_ref[:, lanes] = (part * filtered_ref[group]).astype(BF16)
        grad_filtered_ref[group] = part * query_ref[:, lanes].astype(F32)
    chunk_pass(grad_filtered_ref, rate_ref, entering_ref, total_ref, True)


def share_kernel(weight_hbm, product_ref, keep_ref, send_ref, weight_ref, sem):
    copy = pltpu.make_async_copy(weight_hbm, weight_ref, sem)
    copy.start()
    width = keep_ref.shape[2]
    product = product_ref[...]
    _, _, core = position()
    copy.wait()
    for b in range(keep_ref.shape[0]):
        for out_ref, which in ((send_ref, 1 - core), (keep_ref, core)):
            features = pl.ds(pl.multiple_of((2 * b + which) * width, width), width)
            out_ref[b] = dot(product, weight_ref[:, features], 1, 0).astype(BF16)


def add_kernel(keep_ref, received_ref, *sum_refs):
    chips = len(sum_refs)
    here = lax.axis_index("tp") // 2
    for distance, sum_ref in enumerate(sum_refs):
        b = (here + distance) % chips
        sum_ref[...] = (keep_ref[b].astype(F32) + received_ref[b].astype(F32)).astype(BF16)


def total_kernel(*refs):
    *parts_refs, out_ref = refs
    total = parts_refs[0][...].astype(F32)
    for part_ref in parts_refs[1:]:
        total = total + part_ref[...].astype(F32)
    out_ref[...] = total.astype(out_ref.dtype)


def update_kernel(
    mine_ref, sibling_ref, near_ref, far_ref, product_ref, partner_ref, state_ref, other_state_ref, rate_ref, send_ref
):
    place, half, core = position()
    pairs, channels, _ = mine_ref.shape
    modes = state_ref.shape[0]
    rows = product_ref.shape[1]
    product, partner = product_ref[...], partner_ref[...]
    for b in range(pairs):
        own = jnp.where(core == half, mine_ref[b], sibling_ref[b])
        theirs = jnp.where(core == half, near_ref[b], far_ref[b])
        send_ref[b, :channels, :] = (dot(product, own, 1, 0) + dot(partner, theirs, 1, 0)).astype(BF16)
    rest = pair_total(state_ref[...], other_state_ref[...], rate_ref[...], rows, half, True)
    for part in range(3):
        rounded = rest.astype(BF16)
        rest = rest - rounded.astype(F32)
        for b in range(pairs):
            send_ref[b, channels + part * modes : channels + (part + 1) * modes, :] = rounded


def gather_kernel(parts_ref, out_ref, totals_ref):
    pairs = parts_ref.shape[0]
    channels = out_ref.shape[0]
    modes = totals_ref.shape[1]
    total = parts_ref[0, :channels, :].astype(F32)
    for b in range(1, pairs):
        total = total + parts_ref[b, :channels, :].astype(F32)
    out_ref[...] = total
    for b in range(pairs):
        state = jnp.zeros((modes, out_ref.shape[1]), F32)
        for part in (2, 1, 0):
            state = state + parts_ref[b, channels + part * modes : channels + (part + 1) * modes, :].astype(F32)
        totals_ref[b] = state


def back_kernel(
    key_hbm, value_hbm, rate_ref, coefficient_ref, skip_ref, entering_ref, other_ref, totals_ref, grad_filtered_ref,
    grad_key_ref, grad_value_ref,
    y_ref, incoming_ref, key_ref, value_ref, sems,
):
    copies = start_copies([key_hbm, value_hbm], [key_ref, value_ref], sems)
    rows, channels = key_ref.shape
    place, half, _ = position()
    incoming_ref[...] = incoming_state(totals_ref, other_ref[...], rate_ref[...], rows, place, half, True)
    filter_pass(grad_filtered_ref, y_ref, rate_ref, coefficient_ref, skip_ref, entering_ref, incoming_ref, True)
    for copy in copies:
        copy.wait()
    for group, lanes in lane_groups(channels):
        grad_key_ref[:, lanes] = (y_ref[group] * value_ref[:, lanes].astype(F32)).astype(BF16)
        grad_value_ref[:, lanes] = (y_ref[group] * key_ref[:, lanes].astype(F32)).astype(BF16)


def call(kernel, out_shape, scratch=(), far=0, near=1, after=0, flops=0, bytes_accessed=1 << 20):
    vmem, anywhere = pl.BlockSpec(memory_space=pltpu.VMEM), pl.BlockSpec(memory_space=pl.ANY)
    used = far + near
    return pl.pallas_call(
        lambda *refs: kernel(*refs[:used], *refs[used + after :]),
        out_shape=out_shape,
        in_specs=[anywhere] * far + [vmem] * near + [anywhere] * after,
        out_specs=[vmem] * len(out_shape),
        scratch_shapes=list(scratch),
        compiler_params=pltpu.CompilerParams(vmem_limit_bytes=VMEM_LIMIT),
        cost_estimate=pl.CostEstimate(flops=flops, bytes_accessed=bytes_accessed, transcendentals=0),
    )


def ordered(block, *after):
    anywhere = pl.BlockSpec(memory_space=pl.ANY)
    return pl.pallas_call(
        lambda *refs: None,
        out_shape=jax.ShapeDtypeStruct(block.shape, block.dtype),
        in_specs=[anywhere] * (1 + len(after)),
        out_specs=anywhere,
        input_output_aliases={0: 0},
        compiler_params=pltpu.CompilerParams(vmem_limit_bytes=VMEM_LIMIT),
    )(block, *after)


def on_device(query_feat, key_feat, value_feat, residue, decay_rate, skip_gain, out_weight, cotangent):
    rows, channels = query_feat.shape
    modes = decay_rate.shape[0]
    features = out_weight.shape[1]
    ctx, tp = lax.axis_size("ctx"), lax.axis_size("tp")
    pairs, chips = ctx // 2, tp // 2
    same_core = [[2 * m + c for m in range(chips)] for c in range(2)]
    along_pairs = [[2 * z + h for z in range(pairs)] for h in range(2)]
    siblings = [(i, i ^ 1) for i in range(tp)]
    partners = [(i, i ^ 1) for i in range(ctx)]
    across = [
        ((2 * z + h) * tp + 2 * m + 1 - h, (2 * z + 1 - h) * tp + 2 * m + 1 - h)
        for z in range(pairs) for h in range(2) for m in range(chips)
    ]

    def around(block, distance):
        route = [(2 * m + c, 2 * ((m + distance) % chips) + c) for m in range(chips) for c in range(2)]
        return lax.ppermute(block, "tp", route)

    shape = jax.ShapeDtypeStruct
    block = pltpu.VMEM((channels // LANES, rows, LANES), F32)
    state = pltpu.VMEM((modes, channels), F32)
    plain = pltpu.VMEM((rows, channels), BF16)
    weight = pltpu.VMEM((channels, features), BF16)
    dmas = lambda n: pltpu.SemaphoreType.DMA((n,))
    block_shape = shape((channels // LANES, rows, LANES), F32)
    state_shape = shape((modes, channels), F32)
    totals_shape = shape((pairs, modes, channels), F32)
    entering_shape = shape((modes, CHUNKS, channels), F32)
    small = shape((rows, channels), BF16)
    blocks = shape((chips, rows, channels), BF16)
    matmul_flops = 2 * rows * channels * features
    skip = skip_gain.reshape(1, channels)

    (spread,) = call(spread_kernel, [blocks], [dmas(chips)], far=1, near=0)(cotangent)
    mine = lax.all_to_all(spread, "tp", 0, 0, axis_index_groups=same_core)

    entering, total, coefficient = call(
        signal_kernel,
        [entering_shape, state_shape, state_shape],
        [block, plain, plain, state, state, dmas(4)],
        far=4,
        near=0,
        flops=1 << 25,
    )(key_feat, value_feat, decay_rate, residue)
    other = lax.ppermute(total, "ctx", partners)
    (pair,) = call(lambda *refs: pair_kernel(rows, *refs), [totals_shape], near=3)(total, other, decay_rate)
    mine = ordered(mine, pair)
    near = lax.ppermute(mine, ("ctx", "tp"), across)
    sibling = lax.ppermute(mine, "tp", siblings)
    totals = lax.all_to_all(pair, "ctx", 0, 0, axis_index_groups=along_pairs)

    product, turned, filtered = call(
        forward_kernel,
        [small, shape((channels, rows), BF16), block_shape],
        [block, state, plain, plain, plain, dmas(3)],
        far=3,
        near=6,
        flops=1 << 26,
        bytes_accessed=2 << 20,
    )(query_feat, key_feat, value_feat, decay_rate, coefficient, skip, entering, other, totals)
    turned_other = lax.ppermute(turned, "ctx", partners)
    far = lax.ppermute(ordered(near, product), "tp", siblings)

    grad_query, grad_filtered, back_entering, back_total = call(
        gradient_kernel,
        [small, block_shape, entering_shape, state_shape],
        [plain, weight, dmas(2)],
        far=2,
        near=4,
        flops=matmul_flops + (1 << 25),
        bytes_accessed=6 << 20,
    )(query_feat, out_weight, decay_rate, filtered, mine, sibling)
    back_other = lax.ppermute(back_total, "ctx", partners)

    keep, give = call(
        share_kernel,
        [blocks, blocks],
        [weight, pltpu.SemaphoreType.DMA],
        far=1,
        near=1,
        after=1,
        flops=matmul_flops,
        bytes_accessed=4 << 20,
    )(out_weight, product, back_total)
    taken = lax.ppermute(give, "tp", siblings)

    (update,) = call(
        update_kernel,
        [shape((pairs, channels + 3 * modes, channels), BF16)],
        near=9,
        after=1,
        flops=matmul_flops,
        bytes_accessed=4 << 20,
    )(mine, sibling, near, far, turned, turned_other, back_total, back_other, decay_rate, taken)
    updates = lax.all_to_all(update, "ctx", 0, 0, axis_index_groups=along_pairs)

    own, *sums = call(add_kernel, [small] * chips, near=2, after=1, bytes_accessed=3 << 20)(keep, taken, update)
    shares = [around(part, distance) for distance, part in enumerate(sums, 1)]
    (layer_out,) = call(total_kernel, [small], near=chips, bytes_accessed=2 << 20)(own, *shares)

    grad_out_weight, back_totals = call(
        gather_kernel, [shape((channels, channels), F32), totals_shape], after=1, bytes_accessed=2 << 20
    )(updates, layer_out)
    grad_key, grad_value = call(
        back_kernel,
        [small, small],
        [block, state, plain, plain, dmas(2)],
        far=2,
        near=7,
        flops=1 << 26,
        bytes_accessed=2 << 20,
    )(
        key_feat, value_feat, decay_rate, coefficient, skip, back_entering, back_other, back_totals, grad_filtered
    )
    return (layer_out, grad_query, grad_key, grad_value, grad_out_weight)


def solution(mesh):
    in_specs = (
        P("ctx", "tp"),
        P("ctx", "tp"),
        P("ctx", "tp"),
        P(None, "tp"),
        P(None, "tp"),
        P("tp"),
        P("tp", None),
        P("ctx", "tp"),
    )
    out_specs = (P("ctx", "tp"), P("ctx", "tp"), P("ctx", "tp"), P("ctx", "tp"), P("tp", "ctx"))
    return jax.shard_map(on_device, mesh=mesh, in_specs=in_specs, out_specs=out_specs, check_vma=False)
```

```python
import jax
import jax.numpy as jnp
from jax import lax
from jax.experimental import pallas as pl
from jax.experimental.pallas import tpu as pltpu
from jax.sharding import PartitionSpec as P

CHUNKS = 8
LANES = 128
F32 = jnp.float32
BF16 = jnp.bfloat16
VMEM_LIMIT = 12 * 1024 * 1024


def row_index(shape):
    return lax.broadcasted_iota(jnp.int32, shape, 0)


def lane_groups(channels):
    return [(group, pl.ds(group * LANES, LANES)) for group in range(channels // LANES)]


def one_minus_exp(x):
    series = jnp.ones_like(x)
    for k in range(8, 1, -1):
        series = 1.0 - x / k * series
    return jnp.where(x < 0.3, x * series, 1.0 - jnp.exp(-x))


def chunk_pass(x_ref, rate_ref, entering_ref, total_ref, backward):
    rows = x_ref.shape[1]
    modes, channels = rate_ref.shape
    chunk_len = rows // CHUNKS
    for group, lanes in lane_groups(channels):
        rates = [jnp.broadcast_to(rate_ref[n : n + 1, lanes], (CHUNKS, LANES)) for n in range(modes)]
        decays = [jnp.exp(-rate) for rate in rates]

        def advance(step, states):
            j = chunk_len - 1 - step if backward else step
            x = x_ref[group, pl.ds(j, CHUNKS, stride=chunk_len), :]
            return tuple(d * s + x for d, s in zip(decays, states))

        zero = jnp.zeros((CHUNKS, LANES), F32)
        states = lax.fori_loop(0, chunk_len, advance, (zero,) * modes, unroll=4)
        chunk = row_index((CHUNKS, LANES))
        order = CHUNKS - 1 - chunk if backward else chunk
        for n in range(modes):
            total = states[n]
            span = 1
            while span < CHUNKS:
                earlier = pltpu.roll(total, CHUNKS - span if backward else span, 0)
                across = jnp.exp(-rates[n] * (chunk_len * span))
                total = total + jnp.where(order >= span, across * earlier, 0.0)
                span *= 2
            entering = pltpu.roll(total, CHUNKS - 1 if backward else 1, 0)
            entering_ref[n, :, lanes] = jnp.where(order >= 1, entering, 0.0)
            last = 0 if backward else CHUNKS - 1
            total_ref[n : n + 1, lanes] = total[last : last + 1, :]


def position():
    at_ctx, at_tp = lax.axis_index("ctx"), lax.axis_index("tp")
    return at_ctx // 2, at_ctx % 2, at_tp % 2


def pair_total(total, other, rate, rows, half, backward):
    across = jnp.exp(-rate * rows)
    first = half == (1 if backward else 0)
    return jnp.where(first, across * total + other, across * other + total)


def write_state(ref, row, state):
    modes = state.shape[0]
    high = state.astype(BF16)
    ref[row : row + modes, :] = high
    ref[row + modes : row + 2 * modes, :] = (state - high.astype(F32)).astype(BF16)


def read_state(ref, row, modes):
    return ref[row : row + modes, :].astype(F32) + ref[row + modes : row + 2 * modes, :].astype(F32)


def filter_pass(x_ref, y_ref, rate_ref, coefficient_ref, skip_ref, entering_ref, incoming_ref, backward):
    rows = x_ref.shape[1]
    modes, channels = rate_ref.shape
    chunk_len = rows // CHUNKS
    for group, lanes in lane_groups(channels):
        chunk = row_index((CHUNKS, LANES))
        order = CHUNKS - 1 - chunk if backward else chunk
        start = (order * chunk_len).astype(F32)
        decays, weights, states = [], [], []
        for n in range(modes):
            rate = jnp.broadcast_to(rate_ref[n : n + 1, lanes], (CHUNKS, LANES))
            decays.append(jnp.exp(-rate))
            weights.append(jnp.broadcast_to(coefficient_ref[n : n + 1, lanes], (CHUNKS, LANES)))
            outer = jnp.broadcast_to(incoming_ref[n : n + 1, lanes], (CHUNKS, LANES))
            states.append(entering_ref[n, :, lanes] + jnp.exp(-rate * start) * outer)
        skip = jnp.broadcast_to(skip_ref[0:1, lanes], (CHUNKS, LANES))

        def advance(step, states):
            j = chunk_len - 1 - step if backward else step
            x = x_ref[group, pl.ds(j, CHUNKS, stride=chunk_len), :]
            states = tuple(d * s + x for d, s in zip(decays, states))
            terms = [w * s for w, s in zip(weights, states)] + [skip * x]
            while len(terms) > 1:
                pairs = [terms[i] + terms[i + 1] for i in range(0, len(terms) - 1, 2)]
                terms = pairs + (terms[-1:] if len(terms) % 2 else [])
            y_ref[group, pl.ds(j, CHUNKS, stride=chunk_len), :] = terms[0]
            return states

        lax.fori_loop(0, chunk_len, advance, tuple(states), unroll=2)


def dot(a, b, a_dim, b_dim):
    return lax.dot_general(a, b, (((a_dim,), (b_dim,)), ((), ())), preferred_element_type=F32)


def copies(ref, total_ref):
    for k in range(ref.shape[0]):
        ref[k] = total_ref[...]


def start_copies(sources, targets, sems):
    copies = [pltpu.make_async_copy(a, b, sems.at[i]) for i, (a, b) in enumerate(zip(sources, targets))]
    for copy in copies:
        copy.start()
    return copies


def multiply_signal(x_ref, key, value):
    for group, lanes in lane_groups(key.shape[1]):
        x_ref[group] = key[:, lanes].astype(F32) * value[:, lanes].astype(F32)


def coefficient_of(residue, rate):
    return residue * jnp.sqrt(one_minus_exp(2.0 * rate))


def signal_kernel(
    key_hbm, value_hbm, rate_hbm, cotangent_hbm,
    entering_ref, total_ref, spread_ref,
    x_ref, key_ref, value_ref, rate_ref, cotangent_ref, sems,
):
    copies = start_copies(
        [cotangent_hbm, key_hbm, value_hbm, rate_hbm], [cotangent_ref, key_ref, value_ref, rate_ref], sems
    )
    for copy in copies:
        copy.wait()
    for k in range(spread_ref.shape[0]):
        spread_ref[k] = cotangent_ref[...]
    multiply_signal(x_ref, key_ref, value_ref)
    chunk_pass(x_ref, rate_ref, entering_ref, total_ref, False)


def edge_kernel(rows, total_ref, rate_ref, *refs):
    *behind_refs, edge_ref = refs
    modes = rate_ref.shape[0]
    place, _, _ = position()
    across = jnp.exp(-rate_ref[...] * (2 * rows))
    state = jnp.zeros(rate_ref.shape, F32)
    for behind in range(len(behind_refs), 0, -1):
        state = jnp.where(place >= behind, across * state + behind_refs[behind - 1][...], state)
    edge_ref[:modes, :] = state
    edge_ref[modes:, :] = total_ref[...]


def gradient_kernel(
    query_ref, weight_ref, rate_ref, mine_ref, sibling_ref,
    grad_rows_ref, filtered_hbm, entering_hbm, total_ref,
    grad_filtered_ref, entering_ref, sems,
):
    rows, channels = query_ref.shape
    _, _, core = position()
    grad_rows = jnp.zeros((rows, channels), F32)
    width = mine_ref.shape[2]
    for b in range(mine_ref.shape[0]):
        for block_ref, which in ((mine_ref, core), (sibling_ref, 1 - core)):
            features = weight_ref[:, pl.ds(pl.multiple_of((2 * b + which) * width, width), width)]
            grad_rows = grad_rows + dot(block_ref[b], features, 1, 1)
    for group, lanes in lane_groups(channels):
        part = grad_rows[:, group * LANES : (group + 1) * LANES]
        grad_rows_ref[group] = part
        grad_filtered_ref[group] = part * query_ref[:, lanes].astype(F32)
    out = pltpu.make_async_copy(grad_filtered_ref, filtered_hbm, sems.at[0])
    out.start()
    chunk_pass(grad_filtered_ref, rate_ref, entering_ref, total_ref, True)
    last = pltpu.make_async_copy(entering_ref, entering_hbm, sems.at[1])
    last.start()
    out.wait()
    last.wait()


def forward_kernel(
    query_ref, key_ref, value_ref, rate_ref, residue_ref, skip_ref, entering_ref, weight_ref,
    edge_ref, other_ref, grad_rows_ref, back_total_ref,
    product_hbm, turned_ref, grad_query_ref, send_ref,
    x_ref, y_ref, incoming_ref, product_ref, coefficient_ref, sem,
):
    rows, channels = key_ref.shape
    modes = rate_ref.shape[0]
    _, half, core = position()
    rate = rate_ref[...]
    coefficient_ref[...] = coefficient_of(residue_ref[...], rate)
    across = jnp.exp(-rate * rows)
    edge, other = edge_ref[:modes, :], other_ref[:modes, :]
    incoming_ref[...] = jnp.where(
        half == 0, across * edge + other, across * (across * other + edge) + other_ref[modes:, :]
    )
    multiply_signal(x_ref, key_ref, value_ref)
    filter_pass(x_ref, y_ref, rate_ref, coefficient_ref, skip_ref, entering_ref, incoming_ref, False)
    for group, lanes in lane_groups(channels):
        product = query_ref[:, lanes].astype(F32) * y_ref[group]
        product_ref[:, lanes] = product.astype(BF16)
        turned_ref[lanes, :] = product.T.astype(BF16)
        grad_query_ref[:, lanes] = (grad_rows_ref[group] * y_ref[group]).astype(BF16)
    write_state(turned_ref, channels, back_total_ref[...])
    out = pltpu.make_async_copy(product_ref, product_hbm, sem)
    out.start()
    share(product_ref, weight_ref, send_ref, 1 - core)
    out.wait()


def share(product_ref, weight_ref, out_ref, which):
    width = out_ref.shape[2]
    product = product_ref[...]
    for b in range(out_ref.shape[0]):
        features = pl.ds(pl.multiple_of((2 * b + which) * width, width), width)
        out_ref[b] = dot(product, weight_ref[:, features], 1, 0).astype(BF16)


def add_kernel(product_hbm, weight_hbm, received_hbm, *refs):
    *sum_refs, product_ref, weight_ref, received_ref, sems = refs
    copies = start_copies([product_hbm, received_hbm, weight_hbm], [product_ref, received_ref, weight_ref], sems)
    chips, width = len(sum_refs), sum_refs[0].shape[1]
    here = lax.axis_index("tp") // 2
    _, _, core = position()
    for copy in copies:
        copy.wait()
    product = product_ref[...]
    for distance, sum_ref in enumerate(sum_refs):
        b = (here + distance) % chips
        features = pl.ds(pl.multiple_of((2 * b + core) * width, width), width)
        sum_ref[...] = (dot(product, weight_ref[:, features], 1, 0) + received_ref[b].astype(F32)).astype(BF16)


def total_kernel(*refs):
    *parts_refs, out_ref = refs
    total = parts_refs[0][...].astype(F32)
    for part_ref in parts_refs[1:]:
        total = total + part_ref[...].astype(F32)
    out_ref[...] = total.astype(out_ref.dtype)


def choose_kernel(mine_ref, sibling_ref, out_ref):
    _, half, core = position()
    count = out_ref.shape[0]
    for b in range(count):
        out_ref[b] = jnp.where(core == 1 - half, mine_ref[core * count + b], sibling_ref[core * count + b])


def update_kernel(state_ref, rate_ref, mine_ref, sibling_ref, near_ref, far_ref, product_ref, partner_ref, send_ref):
    place, half, core = position()
    pairs, channels, _ = mine_ref.shape
    modes = state_ref.shape[0]
    rows = product_ref.shape[1]
    count = near_ref.shape[0]
    product, partner = product_ref[:channels, :], partner_ref[:channels, :]
    other = read_state(partner_ref, channels, modes)
    pair = pair_total(state_ref[...], other, rate_ref[...], rows, half, True)
    for b in range(pairs):
        own = jnp.where(core == half, mine_ref[b], sibling_ref[b])
        theirs = jnp.where(core == b // count, near_ref[b % count], far_ref[b % count])
        send_ref[b, :channels, :] = (dot(product, own, 1, 0) + dot(partner, theirs, 1, 0)).astype(BF16)
        write_state(send_ref.at[b], channels, jnp.where(place == b, other, pair))


def back_kernel(
    key_hbm, value_hbm, rate_hbm, residue_hbm, skip_hbm, entering_hbm, grad_filtered_hbm, parts_ref,
    grad_key_ref, grad_value_ref, grad_weight_ref,
    y_ref, incoming_ref, coefficient_ref,
    key_ref, value_ref, rate_ref, residue_ref, skip_ref, entering_ref, grad_filtered_ref, sems,
):
    copies = start_copies(
        [rate_hbm, residue_hbm, skip_hbm, entering_hbm, grad_filtered_hbm, key_hbm, value_hbm],
        [rate_ref, residue_ref, skip_ref, entering_ref, grad_filtered_ref, key_ref, value_ref],
        sems,
    )
    rows, channels = key_ref.shape
    pairs, modes = parts_ref.shape[0], rate_ref.shape[0]
    place, half, _ = position()
    total = parts_ref[0, :channels, :].astype(F32)
    for b in range(1, pairs):
        total = total + parts_ref[b, :channels, :].astype(F32)
    grad_weight_ref[...] = total
    for copy in copies[:-2]:
        copy.wait()
    rate = rate_ref[...]
    coefficient_ref[...] = coefficient_of(residue_ref[...], rate)
    across = jnp.exp(-rate * (2 * rows))
    state = jnp.zeros(rate.shape, F32)
    other = jnp.zeros(rate.shape, F32)
    for k in range(pairs - 1, -1, -1):
        leaves = read_state(parts_ref.at[k], channels, modes)
        state = jnp.where(k > place, across * state + leaves, state)
        other = jnp.where(k == place, leaves, other)
    incoming_ref[...] = jnp.where(half == 1, state, jnp.exp(-rate * rows) * state + other)
    filter_pass(grad_filtered_ref, y_ref, rate_ref, coefficient_ref, skip_ref, entering_ref, incoming_ref, True)
    for copy in copies[-2:]:
        copy.wait()
    for group, lanes in lane_groups(channels):
        grad_key_ref[:, lanes] = (y_ref[group] * value_ref[:, lanes].astype(F32)).astype(BF16)
        grad_value_ref[:, lanes] = (y_ref[group] * key_ref[:, lanes].astype(F32)).astype(BF16)


def call(kernel, out_shape, scratch=(), far=(), fetch=(), near=(), after=(), home=(), hbm=(), flops=0, bytes_accessed=1 << 20):
    vmem, anywhere = pl.BlockSpec(memory_space=pltpu.VMEM), pl.BlockSpec(memory_space=pl.ANY)
    counts = [len(far), len(fetch), len(near), len(after), len(out_shape), len(scratch)]
    edges = [sum(counts[:n]) for n in range(len(counts) + 1)]

    def body(*refs):
        far_refs, fetch_refs, near_refs, _, out_refs, scratch_refs = [
            refs[a:b] for a, b in zip(edges[:-1], edges[1:])
        ]
        own = list(refs[edges[-1] :])
        sems = own.pop() if fetch or home else None
        landed, staged = own[: len(fetch)], dict(zip(home, own[len(fetch) :]))
        for copy in start_copies(fetch_refs, landed, sems):
            copy.wait()
        outs = [staged.get(n, ref) for n, ref in enumerate(out_refs)]
        kernel(*far_refs, *landed, *near_refs, *outs, *scratch_refs)
        for copy in start_copies([staged[n] for n in home], [out_refs[n] for n in home], sems):
            copy.wait()

    extra = [pltpu.VMEM(x.shape, x.dtype) for x in fetch] + [
        pltpu.VMEM(out_shape[n].shape, out_shape[n].dtype) for n in home
    ]
    if extra:
        extra.append(pltpu.SemaphoreType.DMA((max(len(fetch), len(home)),)))
    return pl.pallas_call(
        body,
        out_shape=[pltpu.HBM(x.shape, x.dtype) if n in home or n in hbm else x for n, x in enumerate(out_shape)],
        in_specs=[anywhere] * (len(far) + len(fetch)) + [vmem] * len(near) + [anywhere] * len(after),
        out_specs=[anywhere if n in home or n in hbm else vmem for n in range(len(out_shape))],
        scratch_shapes=list(scratch) + extra,
        compiler_params=pltpu.CompilerParams(vmem_limit_bytes=VMEM_LIMIT),
        cost_estimate=pl.CostEstimate(flops=flops, bytes_accessed=bytes_accessed, transcendentals=0),
    )(*map(in_hbm, far), *map(in_hbm, fetch), *near, *after)


def in_hbm(array):
    return pltpu.with_memory_space_constraint(array, pltpu.HBM)


def ordered(block, *after):
    anywhere = pl.BlockSpec(memory_space=pl.ANY)
    return pl.pallas_call(
        lambda *refs: None,
        out_shape=jax.ShapeDtypeStruct(block.shape, block.dtype),
        in_specs=[anywhere] * (1 + len(after)),
        out_specs=anywhere,
        input_output_aliases={0: 0},
        compiler_params=pltpu.CompilerParams(vmem_limit_bytes=VMEM_LIMIT),
    )(block, *after)


def on_device(query_feat, key_feat, value_feat, residue, decay_rate, skip_gain, out_weight, cotangent):
    rows, channels = query_feat.shape
    modes = decay_rate.shape[0]
    features = out_weight.shape[1]
    ctx, tp = lax.axis_size("ctx"), lax.axis_size("tp")
    pairs, chips = ctx // 2, tp // 2
    same_core = [[2 * m + c for m in range(chips)] for c in range(2)]
    along_pairs = [[2 * z + h for z in range(pairs)] for h in range(2)]
    siblings = [(i, i ^ 1) for i in range(tp)]
    partners = [(i, i ^ 1) for i in range(ctx)]

    def along(block, distance):
        route = [(2 * z + h, 2 * ((z + distance) % pairs) + h) for z in range(pairs) for h in range(2)]
        return lax.ppermute(block, "ctx", route)

    def around(block, distance):
        route = [(2 * m + c, 2 * ((m + distance) % chips) + c) for m in range(chips) for c in range(2)]
        return lax.ppermute(block, "tp", route)

    shape = jax.ShapeDtypeStruct
    block = pltpu.VMEM((channels // LANES, rows, LANES), F32)
    state = pltpu.VMEM((modes, channels), F32)
    plain = pltpu.VMEM((rows, channels), BF16)
    entered = pltpu.VMEM((modes, CHUNKS, channels), F32)
    skips = pltpu.VMEM((1, channels), F32)
    weight = pltpu.VMEM((channels, features), BF16)
    dmas = lambda n: pltpu.SemaphoreType.DMA((n,))
    block_shape = shape((channels // LANES, rows, LANES), F32)
    state_shape = shape((modes, channels), F32)
    entering_shape = shape((modes, CHUNKS, channels), F32)
    small = shape((rows, channels), BF16)
    blocks = shape((chips, rows, channels), BF16)
    matmul_flops = 2 * rows * channels * features
    skip = skip_gain.reshape(1, channels)

    entering, total, spread = call(
        signal_kernel,
        [entering_shape, state_shape, blocks],
        [block, plain, plain, state, plain, dmas(4)],
        far=(key_feat, value_feat, decay_rate, cotangent),
        home=(0,),
        flops=1 << 25,
    )
    mine = lax.all_to_all(spread, "tp", 0, 0, axis_index_groups=same_core)
    behind = [along(total, distance) for distance in range(1, pairs)]
    (edge,) = call(
        lambda *refs: edge_kernel(rows, *refs), [shape((2 * modes, channels), F32)], near=(total, decay_rate, *behind)
    )
    other = lax.ppermute(edge, "ctx", partners)
    mine = ordered(mine, edge)
    sibling = lax.ppermute(mine, "tp", siblings)
    (chosen,) = call(
        choose_kernel, [shape((chips // 2, rows, channels), BF16)], near=(mine, sibling), after=(other,)
    )
    near = lax.ppermute(chosen, "ctx", partners)

    grad_rows, grad_filtered, back_entering, back_total = call(
        gradient_kernel,
        [block_shape, block_shape, entering_shape, state_shape],
        [block, entered, dmas(2)],
        near=(query_feat, out_weight, decay_rate, mine, sibling),
        hbm=(1, 2),
        flops=matmul_flops + (1 << 25),
        bytes_accessed=6 << 20,
    )

    product, turned, grad_query, give = call(
        forward_kernel,
        [small, shape((channels + 2 * modes, rows), BF16), small, blocks],
        [block, block, state, plain, state, pltpu.SemaphoreType.DMA],
        near=(
            query_feat, key_feat, value_feat, decay_rate, residue, skip, entering, out_weight, edge, other, grad_rows,
            back_total,
        ),
        hbm=(0,),
        flops=matmul_flops + (1 << 26),
        bytes_accessed=4 << 20,
    )
    turned_other = lax.ppermute(turned, "ctx", partners)
    near = ordered(near, turned_other)
    far = lax.ppermute(near, "tp", siblings)
    taken = lax.ppermute(give, "tp", siblings)

    (update,) = call(
        update_kernel,
        [shape((pairs, channels + 2 * modes, channels), BF16)],
        near=(back_total, decay_rate, mine, sibling, near, far, turned, turned_other),
        flops=matmul_flops,
        bytes_accessed=4 << 20,
    )
    updates = lax.all_to_all(update, "ctx", 0, 0, axis_index_groups=along_pairs)

    own, *sums = call(
        add_kernel,
        [small] * chips,
        [plain, weight, pltpu.VMEM((chips, rows, channels), BF16), dmas(3)],
        far=(product, out_weight, taken),
        after=(update,),
        flops=matmul_flops // 2,
        bytes_accessed=4 << 20,
    )
    shares = [around(part, distance) for distance, part in enumerate(sums, 1)]
    (layer_out,) = call(total_kernel, [small], near=(own, *shares), bytes_accessed=2 << 20)

    grad_key, grad_value, grad_out_weight = call(
        back_kernel,
        [small, small, shape((channels, channels), F32)],
        [block, state, state, plain, plain, state, state, skips, entered, block, dmas(7)],
        far=(key_feat, value_feat, decay_rate, residue, skip, back_entering, grad_filtered),
        near=(updates,),
        after=(shares[-1],),
        flops=1 << 26,
        bytes_accessed=4 << 20,
    )
    return (layer_out, grad_query, grad_key, grad_value, grad_out_weight)


def solution(mesh):
    in_specs = (
        P("ctx", "tp"),
        P("ctx", "tp"),
        P("ctx", "tp"),
        P(None, "tp"),
        P(None, "tp"),
        P("tp"),
        P("tp", None),
        P("ctx", "tp"),
    )
    out_specs = (P("ctx", "tp"), P("ctx", "tp"), P("ctx", "tp"), P("ctx", "tp"), P("tp", "ctx"))
    return jax.shard_map(on_device, mesh=mesh, in_specs=in_specs, out_specs=out_specs, check_vma=False)
```

```python
import jax
import jax.numpy as jnp
from jax import lax
from jax.experimental import pallas as pl
from jax.experimental.pallas import tpu as pltpu
from jax.sharding import PartitionSpec as P

CHUNKS = 8
LANES = 128
F32 = jnp.float32
BF16 = jnp.bfloat16
VMEM_LIMIT = 12 * 1024 * 1024


def row_index(shape):
    return lax.broadcasted_iota(jnp.int32, shape, 0)


def lane_groups(channels):
    return [(group, pl.ds(group * LANES, LANES)) for group in range(channels // LANES)]


def one_minus_exp(x):
    series = jnp.ones_like(x)
    for k in range(8, 1, -1):
        series = 1.0 - x / k * series
    return jnp.where(x < 0.3, x * series, 1.0 - jnp.exp(-x))


def chunk_pass(x_ref, rate_ref, entering_ref, total_ref, backward):
    rows = x_ref.shape[1]
    modes, channels = rate_ref.shape
    chunk_len = rows // CHUNKS
    for group, lanes in lane_groups(channels):
        rates = [jnp.broadcast_to(rate_ref[n : n + 1, lanes], (CHUNKS, LANES)) for n in range(modes)]
        decays = [jnp.exp(-rate) for rate in rates]

        def advance(step, states):
            j = chunk_len - 1 - step if backward else step
            x = x_ref[group, pl.ds(j, CHUNKS, stride=chunk_len), :]
            return tuple(d * s + x for d, s in zip(decays, states))

        zero = jnp.zeros((CHUNKS, LANES), F32)
        states = lax.fori_loop(0, chunk_len, advance, (zero,) * modes, unroll=4)
        chunk = row_index((CHUNKS, LANES))
        order = CHUNKS - 1 - chunk if backward else chunk
        for n in range(modes):
            total = states[n]
            span = 1
            while span < CHUNKS:
                earlier = pltpu.roll(total, CHUNKS - span if backward else span, 0)
                across = jnp.exp(-rates[n] * (chunk_len * span))
                total = total + jnp.where(order >= span, across * earlier, 0.0)
                span *= 2
            entering = pltpu.roll(total, CHUNKS - 1 if backward else 1, 0)
            entering_ref[n, :, lanes] = jnp.where(order >= 1, entering, 0.0)
            last = 0 if backward else CHUNKS - 1
            total_ref[n : n + 1, lanes] = total[last : last + 1, :]


def position():
    at_ctx, at_tp = lax.axis_index("ctx"), lax.axis_index("tp")
    return at_ctx // 2, at_ctx % 2, at_tp % 2


def pair_total(total, other, rate, rows, half, backward):
    across = jnp.exp(-rate * rows)
    first = half == (1 if backward else 0)
    return jnp.where(first, across * total + other, across * other + total)


def write_state(ref, row, state):
    modes = state.shape[0]
    high = state.astype(BF16)
    ref[row : row + modes, :] = high
    ref[row + modes : row + 2 * modes, :] = (state - high.astype(F32)).astype(BF16)


def read_state(ref, row, modes):
    return ref[row : row + modes, :].astype(F32) + ref[row + modes : row + 2 * modes, :].astype(F32)


def filter_pass(x_ref, y_ref, rate_ref, coefficient_ref, skip_ref, entering_ref, incoming_ref, backward):
    rows = x_ref.shape[1]
    modes, channels = rate_ref.shape
    chunk_len = rows // CHUNKS
    for group, lanes in lane_groups(channels):
        chunk = row_index((CHUNKS, LANES))
        order = CHUNKS - 1 - chunk if backward else chunk
        start = (order * chunk_len).astype(F32)
        decays, weights, states = [], [], []
        for n in range(modes):
            rate = jnp.broadcast_to(rate_ref[n : n + 1, lanes], (CHUNKS, LANES))
            decays.append(jnp.exp(-rate))
            weights.append(jnp.broadcast_to(coefficient_ref[n : n + 1, lanes], (CHUNKS, LANES)))
            outer = jnp.broadcast_to(incoming_ref[n : n + 1, lanes], (CHUNKS, LANES))
            states.append(entering_ref[n, :, lanes] + jnp.exp(-rate * start) * outer)
        skip = jnp.broadcast_to(skip_ref[0:1, lanes], (CHUNKS, LANES))

        def advance(step, states):
            j = chunk_len - 1 - step if backward else step
            x = x_ref[group, pl.ds(j, CHUNKS, stride=chunk_len), :]
            states = tuple(d * s + x for d, s in zip(decays, states))
            terms = [w * s for w, s in zip(weights, states)] + [skip * x]
            while len(terms) > 1:
                pairs = [terms[i] + terms[i + 1] for i in range(0, len(terms) - 1, 2)]
                terms = pairs + (terms[-1:] if len(terms) % 2 else [])
            y_ref[group, pl.ds(j, CHUNKS, stride=chunk_len), :] = terms[0]
            return states

        lax.fori_loop(0, chunk_len, advance, tuple(states), unroll=2)


def dot(a, b, a_dim, b_dim):
    return lax.dot_general(a, b, (((a_dim,), (b_dim,)), ((), ())), preferred_element_type=F32)


def copies(ref, total_ref):
    for k in range(ref.shape[0]):
        ref[k] = total_ref[...]


def start_copies(sources, targets, sems):
    copies = [pltpu.make_async_copy(a, b, sems.at[i]) for i, (a, b) in enumerate(zip(sources, targets))]
    for copy in copies:
        copy.start()
    return copies


def multiply_signal(x_ref, key, value):
    for group, lanes in lane_groups(key.shape[1]):
        x_ref[group] = key[:, lanes].astype(F32) * value[:, lanes].astype(F32)


def coefficient_of(residue, rate):
    return residue * jnp.sqrt(one_minus_exp(2.0 * rate))


def signal_kernel(
    key_hbm, value_hbm, rate_hbm, cotangent_hbm,
    entering_ref, total_ref, spread_ref,
    x_ref, key_ref, value_ref, rate_ref, cotangent_ref, sems,
):
    copies = start_copies(
        [cotangent_hbm, key_hbm, value_hbm, rate_hbm], [cotangent_ref, key_ref, value_ref, rate_ref], sems
    )
    for copy in copies:
        copy.wait()
    for k in range(spread_ref.shape[0]):
        spread_ref[k] = cotangent_ref[...]
    multiply_signal(x_ref, key_ref, value_ref)
    chunk_pass(x_ref, rate_ref, entering_ref, total_ref, False)


def edge_kernel(rows, total_ref, rate_ref, *refs):
    *behind_refs, edge_ref = refs
    modes = rate_ref.shape[0]
    place, _, _ = position()
    across = jnp.exp(-rate_ref[...] * (2 * rows))
    state = jnp.zeros(rate_ref.shape, F32)
    for behind in range(len(behind_refs), 0, -1):
        state = jnp.where(place >= behind, across * state + behind_refs[behind - 1][...], state)
    edge_ref[:modes, :] = state
    edge_ref[modes:, :] = total_ref[...]


def gradient_kernel(
    query_ref, weight_ref, rate_ref, mine_ref, sibling_ref,
    grad_rows_ref, filtered_hbm, entering_hbm, total_ref,
    grad_filtered_ref, entering_ref, sems,
):
    rows, channels = query_ref.shape
    _, _, core = position()
    grad_rows = jnp.zeros((rows, channels), F32)
    width = mine_ref.shape[2]
    for b in range(mine_ref.shape[0]):
        for block_ref, which in ((mine_ref, core), (sibling_ref, 1 - core)):
            features = weight_ref[:, pl.ds(pl.multiple_of((2 * b + which) * width, width), width)]
            grad_rows = grad_rows + dot(block_ref[b], features, 1, 1)
    for group, lanes in lane_groups(channels):
        part = grad_rows[:, group * LANES : (group + 1) * LANES]
        grad_rows_ref[group] = part
        grad_filtered_ref[group] = part * query_ref[:, lanes].astype(F32)
    out = pltpu.make_async_copy(grad_filtered_ref, filtered_hbm, sems.at[0])
    out.start()
    chunk_pass(grad_filtered_ref, rate_ref, entering_ref, total_ref, True)
    last = pltpu.make_async_copy(entering_ref, entering_hbm, sems.at[1])
    last.start()
    out.wait()
    last.wait()


def forward_kernel(
    query_ref, key_ref, value_ref, rate_ref, residue_ref, skip_ref, entering_ref,
    edge_ref, other_ref, grad_rows_ref, back_total_ref,
    product_hbm, turned_ref, grad_query_ref,
    x_ref, y_ref, incoming_ref, product_ref, coefficient_ref, sem,
):
    rows, channels = key_ref.shape
    modes = rate_ref.shape[0]
    _, half, core = position()
    rate = rate_ref[...]
    coefficient_ref[...] = coefficient_of(residue_ref[...], rate)
    across = jnp.exp(-rate * rows)
    edge, other = edge_ref[:modes, :], other_ref[:modes, :]
    incoming_ref[...] = jnp.where(
        half == 0, across * edge + other, across * (across * other + edge) + other_ref[modes:, :]
    )
    multiply_signal(x_ref, key_ref, value_ref)
    filter_pass(x_ref, y_ref, rate_ref, coefficient_ref, skip_ref, entering_ref, incoming_ref, False)
    for group, lanes in lane_groups(channels):
        product = query_ref[:, lanes].astype(F32) * y_ref[group]
        product_ref[:, lanes] = product.astype(BF16)
        turned_ref[lanes, :] = product.T.astype(BF16)
        grad_query_ref[:, lanes] = (grad_rows_ref[group] * y_ref[group]).astype(BF16)
    write_state(turned_ref, channels, back_total_ref[...])
    out = pltpu.make_async_copy(product_ref, product_hbm, sem)
    out.start()
    out.wait()


def share(product_ref, weight_ref, out_ref, which):
    width = out_ref.shape[2]
    product = product_ref[...]
    for b in range(out_ref.shape[0]):
        features = pl.ds(pl.multiple_of((2 * b + which) * width, width), width)
        out_ref[b] = dot(product, weight_ref[:, features], 1, 0).astype(BF16)


def share_kernel(product_hbm, weight_hbm, send_ref, product_ref, weight_ref, sems):
    for copy in start_copies([product_hbm, weight_hbm], [product_ref, weight_ref], sems):
        copy.wait()
    _, _, core = position()
    share(product_ref, weight_ref, send_ref, 1 - core)


def add_kernel(product_hbm, weight_hbm, received_hbm, *refs):
    *sum_refs, product_ref, weight_ref, received_ref, sems = refs
    copies = start_copies([product_hbm, received_hbm, weight_hbm], [product_ref, received_ref, weight_ref], sems)
    chips, width = len(sum_refs), sum_refs[0].shape[1]
    here = lax.axis_index("tp") // 2
    _, _, core = position()
    for copy in copies:
        copy.wait()
    product = product_ref[...]
    for distance, sum_ref in enumerate(sum_refs):
        b = (here + distance) % chips
        features = pl.ds(pl.multiple_of((2 * b + core) * width, width), width)
        sum_ref[...] = (dot(product, weight_ref[:, features], 1, 0) + received_ref[b].astype(F32)).astype(BF16)


def total_kernel(*refs):
    *parts_refs, out_ref = refs
    total = parts_refs[0][...].astype(F32)
    for part_ref in parts_refs[1:]:
        total = total + part_ref[...].astype(F32)
    out_ref[...] = total.astype(out_ref.dtype)


def each_place(body):
    _, half, core = position()
    for c in range(2):
        for h in range(2):
            pl.when((core == c) & (half == h))(lambda c=c, h=h: body(c, h))


def choose_kernel(part, mine_ref, sibling_ref, out_ref):
    count = out_ref.shape[0]

    def choose(core, half):
        source_ref = mine_ref if core == 1 - half else sibling_ref
        first = (2 * core + part) * count
        out_ref[...] = source_ref[first : first + count]

    each_place(choose)


def update_kernel(
    state_ref, rate_ref, mine_ref, sibling_ref, near_0_ref, near_1_ref, far_0_ref, far_1_ref, product_ref, partner_ref,
    send_ref,
):
    place, half, _ = position()
    pairs, channels, _ = mine_ref.shape
    modes = state_ref.shape[0]
    rows = product_ref.shape[1]
    count = near_0_ref.shape[0]
    product, partner = product_ref[:channels, :], partner_ref[:channels, :]
    other = read_state(partner_ref, channels, modes)
    pair = pair_total(state_ref[...], other, rate_ref[...], rows, half, True)
    for b in range(pairs):
        write_state(send_ref.at[b], channels, jnp.where(place == b, other, pair))

    def add_up(core, half):
        own_ref = mine_ref if core == half else sibling_ref
        for b in range(pairs):
            near_ref, far_ref = ((near_0_ref, far_0_ref), (near_1_ref, far_1_ref))[b // count % 2]
            theirs_ref = near_ref if core == b // count // 2 else far_ref
            block = dot(product, own_ref[b], 1, 0) + dot(partner, theirs_ref[b % count], 1, 0)
            send_ref[b, :channels, :] = block.astype(BF16)

    each_place(add_up)


def back_kernel(
    key_hbm, value_hbm, rate_hbm, residue_hbm, skip_hbm, entering_hbm, grad_filtered_hbm, parts_ref,
    grad_key_ref, grad_value_ref, grad_weight_ref,
    y_ref, incoming_ref, coefficient_ref,
    key_ref, value_ref, rate_ref, residue_ref, skip_ref, entering_ref, grad_filtered_ref, sems,
):
    copies = start_copies(
        [rate_hbm, residue_hbm, skip_hbm, entering_hbm, grad_filtered_hbm, key_hbm, value_hbm],
        [rate_ref, residue_ref, skip_ref, entering_ref, grad_filtered_ref, key_ref, value_ref],
        sems,
    )
    rows, channels = key_ref.shape
    pairs, modes = parts_ref.shape[0], rate_ref.shape[0]
    place, half, _ = position()
    total = parts_ref[0, :channels, :].astype(F32)
    for b in range(1, pairs):
        total = total + parts_ref[b, :channels, :].astype(F32)
    grad_weight_ref[...] = total
    for copy in copies[:-2]:
        copy.wait()
    rate = rate_ref[...]
    coefficient_ref[...] = coefficient_of(residue_ref[...], rate)
    across = jnp.exp(-rate * (2 * rows))
    state = jnp.zeros(rate.shape, F32)
    other = jnp.zeros(rate.shape, F32)
    for k in range(pairs - 1, -1, -1):
        leaves = read_state(parts_ref.at[k], channels, modes)
        state = jnp.where(k > place, across * state + leaves, state)
        other = jnp.where(k == place, leaves, other)
    incoming_ref[...] = jnp.where(half == 1, state, jnp.exp(-rate * rows) * state + other)
    filter_pass(grad_filtered_ref, y_ref, rate_ref, coefficient_ref, skip_ref, entering_ref, incoming_ref, True)
    for copy in copies[-2:]:
        copy.wait()
    for group, lanes in lane_groups(channels):
        grad_key_ref[:, lanes] = (y_ref[group] * value_ref[:, lanes].astype(F32)).astype(BF16)
        grad_value_ref[:, lanes] = (y_ref[group] * key_ref[:, lanes].astype(F32)).astype(BF16)


def call(kernel, out_shape, scratch=(), far=(), fetch=(), near=(), after=(), home=(), hbm=(), flops=0, bytes_accessed=1 << 20):
    vmem, anywhere = pl.BlockSpec(memory_space=pltpu.VMEM), pl.BlockSpec(memory_space=pl.ANY)
    counts = [len(far), len(fetch), len(near), len(after), len(out_shape), len(scratch)]
    edges = [sum(counts[:n]) for n in range(len(counts) + 1)]

    def body(*refs):
        far_refs, fetch_refs, near_refs, _, out_refs, scratch_refs = [
            refs[a:b] for a, b in zip(edges[:-1], edges[1:])
        ]
        own = list(refs[edges[-1] :])
        sems = own.pop() if fetch or home else None
        landed, staged = own[: len(fetch)], dict(zip(home, own[len(fetch) :]))
        for copy in start_copies(fetch_refs, landed, sems):
            copy.wait()
        outs = [staged.get(n, ref) for n, ref in enumerate(out_refs)]
        kernel(*far_refs, *landed, *near_refs, *outs, *scratch_refs)
        for copy in start_copies([staged[n] for n in home], [out_refs[n] for n in home], sems):
            copy.wait()

    extra = [pltpu.VMEM(x.shape, x.dtype) for x in fetch] + [
        pltpu.VMEM(out_shape[n].shape, out_shape[n].dtype) for n in home
    ]
    if extra:
        extra.append(pltpu.SemaphoreType.DMA((max(len(fetch), len(home)),)))
    return pl.pallas_call(
        body,
        out_shape=[pltpu.HBM(x.shape, x.dtype) if n in home or n in hbm else x for n, x in enumerate(out_shape)],
        in_specs=[anywhere] * (len(far) + len(fetch)) + [vmem] * len(near) + [anywhere] * len(after),
        out_specs=[anywhere if n in home or n in hbm else vmem for n in range(len(out_shape))],
        scratch_shapes=list(scratch) + extra,
        compiler_params=pltpu.CompilerParams(vmem_limit_bytes=VMEM_LIMIT),
        cost_estimate=pl.CostEstimate(flops=flops, bytes_accessed=bytes_accessed, transcendentals=0),
    )(*map(in_hbm, far), *map(in_hbm, fetch), *near, *after)


def in_hbm(array):
    return pltpu.with_memory_space_constraint(array, pltpu.HBM)


def ordered(block, *after):
    anywhere = pl.BlockSpec(memory_space=pl.ANY)
    return pl.pallas_call(
        lambda *refs: None,
        out_shape=jax.ShapeDtypeStruct(block.shape, block.dtype),
        in_specs=[anywhere] * (1 + len(after)),
        out_specs=anywhere,
        input_output_aliases={0: 0},
        compiler_params=pltpu.CompilerParams(vmem_limit_bytes=VMEM_LIMIT),
    )(block, *after)


def on_device(query_feat, key_feat, value_feat, residue, decay_rate, skip_gain, out_weight, cotangent):
    rows, channels = query_feat.shape
    modes = decay_rate.shape[0]
    features = out_weight.shape[1]
    ctx, tp = lax.axis_size("ctx"), lax.axis_size("tp")
    pairs, chips = ctx // 2, tp // 2
    same_core = [[2 * m + c for m in range(chips)] for c in range(2)]
    along_pairs = [[2 * z + h for z in range(pairs)] for h in range(2)]
    siblings = [(i, i ^ 1) for i in range(tp)]
    partners = [(i, i ^ 1) for i in range(ctx)]

    def along(block, distance):
        route = [(2 * z + h, 2 * (z + distance) + h) for z in range(pairs - distance) for h in range(2)]
        return lax.ppermute(block, "ctx", route)

    def around(block, distance):
        route = [(2 * m + c, 2 * ((m + distance) % chips) + c) for m in range(chips) for c in range(2)]
        return lax.ppermute(block, "tp", route)

    shape = jax.ShapeDtypeStruct
    block = pltpu.VMEM((channels // LANES, rows, LANES), F32)
    state = pltpu.VMEM((modes, channels), F32)
    plain = pltpu.VMEM((rows, channels), BF16)
    entered = pltpu.VMEM((modes, CHUNKS, channels), F32)
    skips = pltpu.VMEM((1, channels), F32)
    weight = pltpu.VMEM((channels, features), BF16)
    dmas = lambda n: pltpu.SemaphoreType.DMA((n,))
    block_shape = shape((channels // LANES, rows, LANES), F32)
    state_shape = shape((modes, channels), F32)
    entering_shape = shape((modes, CHUNKS, channels), F32)
    small = shape((rows, channels), BF16)
    blocks = shape((chips, rows, channels), BF16)
    matmul_flops = 2 * rows * channels * features
    skip = skip_gain.reshape(1, channels)

    entering, total, spread = call(
        signal_kernel,
        [entering_shape, state_shape, blocks],
        [block, plain, plain, state, plain, dmas(4)],
        far=(key_feat, value_feat, decay_rate, cotangent),
        flops=1 << 25,
    )
    mine = lax.all_to_all(spread, "tp", 0, 0, axis_index_groups=same_core)
    behind = [along(total, distance) for distance in range(1, pairs)]
    (edge,) = call(
        lambda *refs: edge_kernel(rows, *refs), [shape((2 * modes, channels), F32)], near=(total, decay_rate, *behind)
    )
    other = lax.ppermute(edge, "ctx", partners)
    mine = ordered(mine, edge)
    sibling = lax.ppermute(mine, "tp", siblings)
    quarter = shape((chips // 4, rows, channels), BF16)
    (chosen,) = call(lambda *refs: choose_kernel(0, *refs), [quarter], near=(mine, sibling))
    near_0 = lax.ppermute(chosen, "ctx", partners)
    (chosen,) = call(lambda *refs: choose_kernel(1, *refs), [quarter], near=(mine, sibling), after=(other,))
    near_1 = lax.ppermute(chosen, "ctx", partners)

    grad_rows, grad_filtered, back_entering, back_total = call(
        gradient_kernel,
        [block_shape, block_shape, entering_shape, state_shape],
        [block, entered, dmas(2)],
        near=(query_feat, out_weight, decay_rate, mine, sibling),
        hbm=(1, 2),
        flops=matmul_flops + (1 << 25),
        bytes_accessed=6 << 20,
    )

    product, turned, grad_query = call(
        forward_kernel,
        [small, shape((channels + 2 * modes, rows), BF16), small],
        [block, block, state, plain, state, pltpu.SemaphoreType.DMA],
        near=(
            query_feat, key_feat, value_feat, decay_rate, residue, skip, entering, edge, other, grad_rows,
            back_total,
        ),
        hbm=(0,),
        flops=1 << 26,
        bytes_accessed=2 << 20,
    )
    turned_other = lax.ppermute(turned, "ctx", partners)
    near_0 = ordered(near_0, in_hbm(product))
    far_0 = lax.ppermute(near_0, "tp", siblings)
    near_1 = ordered(near_1, turned_other)
    far_1 = lax.ppermute(near_1, "tp", siblings)

    (update,) = call(
        update_kernel,
        [shape((pairs, channels + 2 * modes, channels), BF16)],
        near=(back_total, decay_rate, mine, sibling, near_0, near_1, far_0, far_1, turned, turned_other),
        flops=matmul_flops,
        bytes_accessed=4 << 20,
    )
    updates = lax.all_to_all(update, "ctx", 0, 0, axis_index_groups=along_pairs)

    (give,) = call(
        share_kernel,
        [blocks],
        [plain, weight, dmas(2)],
        far=(product, out_weight),
        after=(update,),
        flops=matmul_flops // 2,
        bytes_accessed=4 << 20,
    )
    taken = lax.ppermute(give, "tp", siblings)
    own, *sums = call(
        add_kernel,
        [small] * chips,
        [plain, weight, pltpu.VMEM((chips, rows, channels), BF16), dmas(3)],
        far=(product, out_weight, taken),
        after=(update,),
        flops=matmul_flops // 2,
        bytes_accessed=4 << 20,
    )
    shares = [around(part, distance) for distance, part in enumerate(sums, 1)]
    (layer_out,) = call(total_kernel, [small], near=(own, *shares), bytes_accessed=2 << 20)

    grad_key, grad_value, grad_out_weight = call(
        back_kernel,
        [small, small, shape((channels, channels), F32)],
        [block, state, state, plain, plain, state, state, skips, entered, block, dmas(7)],
        far=(key_feat, value_feat, decay_rate, residue, skip, back_entering, grad_filtered),
        near=(updates,),
        after=(shares[-1],),
        flops=1 << 26,
        bytes_accessed=4 << 20,
    )
    return (layer_out, grad_query, grad_key, grad_value, grad_out_weight)


def solution(mesh):
    in_specs = (
        P("ctx", "tp"),
        P("ctx", "tp"),
        P("ctx", "tp"),
        P(None, "tp"),
        P(None, "tp"),
        P("tp"),
        P("tp", None),
        P("ctx", "tp"),
    )
    out_specs = (P("ctx", "tp"), P("ctx", "tp"), P("ctx", "tp"), P("ctx", "tp"), P("tp", "ctx"))
    return jax.shard_map(on_device, mesh=mesh, in_specs=in_specs, out_specs=out_specs, check_vma=False)
```
